512 devices in a mesh: gx: 32 (over z_lo, y), gy: 16 (over x, z_hi, core).
Axes of the slice: x: 4, y: 4, z: 16 (z_hi: 2, z_lo: 8; z = z_hi * 8 + z_lo), core: 2. Of those that a mesh axis runs over, the one named last changes fastest.
Arguments:
- image_embeds: bfloat16 [49152, 1152], P(('gx', 'gy')), may hold values from -0.75 to 0.75
- text_embeds: bfloat16 [49152, 1152], P(('gx', 'gy')), may hold values from -0.75 to 0.75
- logit_scale: float32 [1], replicated, may hold values from 4 to 8
- logit_bias: float32 [1], replicated, may hold values from -3 to -1
Outputs:
- image_grads: float32 [49152, 1152], P(('gx', 'gy'))
- text_grads: float32 [49152, 1152], P(('gx', 'gy'))
The draws below stay inside these ranges and needn't reach their ends.
All inputs are finite; a program needn't handle non-finite values.
Results may differ from the reference program's by a relative error of at most 0.003.
Values may be sent and summed in bfloat16 or wider, within the bound.
A program may use at most 64 MiB of HBM per device.

```python
import math
import jax
import jax.numpy as jnp
from jax import lax

D = 1152
PAIRS_DEV = 96
REACH = 1
PAIRS = 49152
N_GX = 32
N_GY = 16


def level_of(rng, dims, cuts, smallest, top_value):
    loudness = 1.0
    for axis_at, parts in cuts:
        draws = jax.random.uniform(jax.random.fold_in(jax.random.fold_in(rng, 6), axis_at), (parts,), jnp.float32, smallest / len(cuts), top_value / len(cuts))
        loudness = loudness * jnp.repeat(jnp.exp(draws), dims[axis_at] // parts).reshape((-1,) + (1,) * (len(dims) - 1 - axis_at))
    return loudness


def normal_values(key, extent, deviation, most, shards=(), held_as=jnp.bfloat16):
    level = level_of(key, extent, shards, -0.22, 0.18) if shards else 1.0
    values = jax.random.normal(key, extent, jnp.float32) * deviation * level
    return jnp.minimum(jnp.maximum(values, -most), most).astype(held_as)


def setup_inputs(seed: int = 0) -> dict:
    key_list = jax.random.split(jax.random.key(seed), 5)
    return {
        "image_embeds": normal_values(key_list[0], (PAIRS, D), 0.05, 0.75, ((0, 512),)),
        "text_embeds": normal_values(key_list[1], (PAIRS, D), 0.05, 0.75, ((0, 512),)),
        "logit_scale": jnp.clip(jnp.exp(jax.random.uniform(key_list[2], (1,), jnp.float32, math.log(4.0), math.log(8.0))), 4.0, 8.0),
        "logit_bias": jnp.clip(jax.random.uniform(key_list[3], (1,), jnp.float32, -3.0, -1.0), -3.0, -1.0),
    }


def reference(image_embeds, text_embeds, logit_scale, logit_bias):
    gain = logit_scale[0]
    offset = logit_bias[0]
    group_rows = N_GY * PAIRS_DEV
    width = image_embeds.shape[1]
    image_groups = image_embeds.reshape(N_GX, group_rows, width)
    text_groups = text_embeds.reshape(N_GX, N_GY, PAIRS_DEV, width)
    row_ids = jnp.arange(group_rows, dtype=jnp.int32)
    text_local = jnp.arange(N_GY, dtype=jnp.int32)[:, None] * PAIRS_DEV + jnp.arange(PAIRS_DEV, dtype=jnp.int32)[None, :]
    labels_home = (text_local[:, :, None] == row_ids[None, None, :]).astype(jnp.float32)

    def visit(text_total, group):
        images = lax.dynamic_index_in_dim(image_groups, group, 0, keepdims=False).astype(jnp.float32)
        partial_value = jnp.zeros((N_GY, group_rows, width), jnp.float32)
        for step in range(-REACH, REACH + 1):
            source = ((group - step) % N_GX).astype(jnp.int32)
            texts = lax.dynamic_index_in_dim(text_groups, source, 0, keepdims=False).astype(jnp.float32)
            products = jnp.einsum("ypd,rd->ypr", texts, images)
            logits = gain * products + offset
            if step == 0:
                weights = (jax.nn.sigmoid(logits) - labels_home).astype(jnp.bfloat16)
            else:
                weights = jax.nn.sigmoid(logits).astype(jnp.bfloat16)
            wide = weights.astype(jnp.float32)
            text_part = jnp.einsum("ypr,rd->ypd", wide, images)
            current = lax.dynamic_index_in_dim(text_total, source, 0, keepdims=False)
            text_total = lax.dynamic_update_index_in_dim(text_total, current + text_part, source, 0)
            partial_value = partial_value + jnp.einsum("ypr,ypd->yrd", wide, texts)
        rounded = lax.optimization_barrier(partial_value.astype(jnp.bfloat16))
        image_part = jnp.sum(rounded.astype(jnp.float32), axis=0)
        return text_total, image_part

    start_total = jnp.zeros((N_GX, N_GY, PAIRS_DEV, width), jnp.float32)
    groups = jnp.arange(N_GX, dtype=jnp.int32)
    text_total, image_parts = lax.scan(visit, start_total, groups)
    total_rows = image_embeds.shape[0]
    return gain * image_parts.reshape(total_rows, width), gain * text_total.reshape(total_rows, width)
```

```python
import jax
import jax.numpy as jnp
from jax import lax
from jax.experimental import pallas as pl
from jax.experimental.pallas import tpu as pltpu
from jax.sharding import PartitionSpec as P

MESH = pl.DeviceIdType.MESH
CHUNKS = (32, 32, 32)
CHIPS_X = 4
NT = (((1,), (1,)), ((), ()))
TN = (((0,), (0,)), ((), ()))


def kernel(
    gain_ref, bias_ref, image_ref, text_ref,
    image_out, text_out,
    texts, near, far, text_sum, text_in, text_send, text_back,
    near_own, near_send, near_in, far_own, far_send, far_in, back_send, back_in,
    send_sems, recv_sems, local_sems,
):
    rows, width = image_ref.shape
    group_count = lax.axis_size("gx")
    plane_count = 2 * group_count
    here_x = lax.axis_index("gx")
    here_y = lax.axis_index("gy")
    core = here_y % 2
    chip = here_y // 4
    plane = here_x + group_count * ((here_y // 2) % 2)

    def device(plane_step, chip_step, other_core=False):
        to_plane = (plane + plane_step + plane_count) % plane_count
        to_chip = (chip + chip_step) % CHIPS_X
        to_core = 1 - core if other_core else core
        return (to_plane % group_count, to_chip * 4 + (to_plane // group_count) * 2 + to_core)

    mate = device(0, 0, True)
    across = device(group_count, 0)
    above = device(1, 0)
    below = device(-1, 0)
    side = {step: device(0, step) for step in (1, 3, 2)}

    barrier = pltpu.get_barrier_semaphore()
    partners = [across, above, below, side[1], side[2], side[3], mate]
    for partner in partners:
        pl.semaphore_signal(barrier, inc=1, device_id=partner, device_id_type=MESH)

    used = [0]
    started = []

    def send(source, target, to):
        slot = used[0]
        used[0] += 1
        copy = pltpu.make_async_remote_copy(
            src_ref=source, dst_ref=target, send_sem=send_sems.at[slot], recv_sem=recv_sems.at[slot],
            device_id=to, device_id_type=MESH,
        )
        copy.start()
        started.append(copy)
        return copy

    def block(ref, at, count=rows):
        return ref.at[pl.ds(at, count)]

    starts = [sum(CHUNKS[:k]) for k in range(len(CHUNKS))]
    own_text = pltpu.make_async_copy(text_ref, block(texts, 0), local_sems.at[0])
    own_image = pltpu.make_async_copy(image_ref, block(near, 0), local_sems.at[1])
    own_text.start()
    own_image.start()
    pl.semaphore_wait(barrier, len(partners))

    outward = [
        send(block(image_ref, at, count), block(far, 4 * at, count), across)
        for at, count in zip(starts, CHUNKS)
    ]
    up = send(text_ref, block(texts, 2 * rows), above)
    down = send(text_ref, block(texts, rows), below)
    to_mate = send(text_ref, block(texts, 3 * rows), mate)
    spread = [send(image_ref, block(near, (4 - step) * rows), side[step]) for step in side]

    up.wait_recv()
    passed_up = send(block(texts, 2 * rows), block(texts, 5 * rows), mate)
    down.wait_recv()
    passed_down = send(block(texts, rows), block(texts, 4 * rows), mate)

    gathers = {}

    def gather(k):
        at, count = starts[k], CHUNKS[k]
        outward[k].wait_recv()
        gathers[k] = [
            send(block(far, 4 * at, count), block(far, 4 * at + (4 - step) * count, count), side[step])
            for step in side
        ]

    gain = gain_ref[0]
    bias = bias_ref[0]

    def weights_of(images, own):
        logits = lax.dot_general(images, texts[...], NT, preferred_element_type=jnp.float32)
        weights = jax.nn.sigmoid(gain * logits + bias)
        if own:
            row = lax.broadcasted_iota(jnp.int32, logits.shape, 0)
            column = lax.broadcasted_iota(jnp.int32, logits.shape, 1)
            weights = weights - jnp.logical_and(row == column, row < rows).astype(jnp.float32)
        return weights.astype(jnp.bfloat16)

    gather(0)
    own_text.wait()
    own_image.wait()
    for copy in spread + [to_mate, passed_up, passed_down]:
        copy.wait_recv()

    images = near[...]
    weights = weights_of(images, True)
    text_sum[...] = lax.dot_general(weights, images, TN, preferred_element_type=jnp.float32)
    partial = jnp.dot(weights, texts[...], preferred_element_type=jnp.float32)
    near_own[...] = partial[:rows]
    near_send[...] = partial[rows:].astype(jnp.bfloat16)

    scatters = {}
    returns = {}

    def work(k):
        at, count = starts[k], CHUNKS[k]
        for copy in gathers[k]:
            copy.wait_recv()
        images = far[pl.ds(4 * at, 4 * count), :]
        weights = weights_of(images, False)
        partial = jnp.dot(weights, texts[...], preferred_element_type=jnp.float32)
        far_own[pl.ds(at, count), :] = partial[:count]
        far_send[pl.ds(3 * at, 3 * count), :] = partial[count:].astype(jnp.bfloat16)
        scatters[k] = [
            send(
                block(far_send, 3 * at + (step - 1) * count, count),
                block(far_in, 3 * at + (3 - step) * count, count),
                side[step],
            )
            for step in side
        ]
        text_sum[...] += lax.dot_general(weights, images, TN, preferred_element_type=jnp.float32)

    def give_back(k):
        at, count = starts[k], CHUNKS[k]
        for copy in scatters[k]:
            copy.wait_recv()
        total = far_own[pl.ds(at, count), :]
        for step in range(3):
            total = total + far_in[pl.ds(3 * at + step * count, count), :].astype(jnp.float32)
        back_send[pl.ds(at, count), :] = total.astype(jnp.bfloat16)
        returns[k] = send(block(back_send, at, count), block(back_in, at, count), across)

    last = len(CHUNKS) - 1
    if last >= 1:
        gather(1)
    for k in range(last + 1):
        work(k)
        if k + 2 <= last:
            gather(k + 2)
        if k >= 1:
            give_back(k - 1)
    to_core = send(block(text_sum, 3 * rows, 3 * rows), text_in, mate)
    near_scatter = [
        send(block(near_send, (step - 1) * rows), block(near_in, (3 - step) * rows), side[step]) for step in side
    ]
    give_back(last)

    to_core.wait_recv()
    for step in (0, 1):
        part = pl.ds((step + 1) * rows, rows)
        text_send[pl.ds(step * rows, rows), :] = (text_sum[part, :] + text_in[part, :]).astype(jnp.bfloat16)
    text_up = send(block(text_send, 0), block(text_back, 0), above)
    text_down = send(block(text_send, rows), block(text_back, rows), below)

    for copy in near_scatter:
        copy.wait_recv()
    total = near_own[...]
    for step in range(3):
        total = total + near_in[pl.ds(step * rows, rows), :].astype(jnp.float32)
    near_own[...] = total

    text_up.wait_recv()
    text_down.wait_recv()
    text_out[...] = (
        text_sum[pl.ds(0, rows), :]
        + text_in[pl.ds(0, rows), :]
        + text_back[pl.ds(0, rows), :].astype(jnp.float32)
        + text_back[pl.ds(rows, rows), :].astype(jnp.float32)
    )
    for k in range(last + 1):
        part = pl.ds(starts[k], CHUNKS[k])
        returns[k].wait_recv()
        image_out[part, :] = near_own[part, :] + back_in[part, :].astype(jnp.float32)
    for copy in started:
        copy.wait_send()


def body(image_embeds, text_embeds, logit_scale, logit_bias):
    rows, width = image_embeds.shape
    copies = 1 * len(CHUNKS) + 3 + 3 + 2 + 3 * len(CHUNKS) * 2 + len(CHUNKS) + 1 + 3 + 2
    half = lambda count: pltpu.VMEM((count * rows, width), jnp.bfloat16)
    full = lambda count: pltpu.VMEM((count * rows, width), jnp.float32)
    smem = pl.BlockSpec(memory_space=pltpu.SMEM)
    anywhere = pl.BlockSpec(memory_space=pl.ANY)
    vmem = pl.BlockSpec(memory_space=pltpu.VMEM)
    image_total, text_total = pl.pallas_call(
        kernel,
        out_shape=[jax.ShapeDtypeStruct((rows, width), jnp.float32)] * 2,
        in_specs=[smem, smem, anywhere, anywhere],
        out_specs=[vmem, vmem],
        scratch_shapes=[
            half(6), half(4), half(4), full(6), full(3), half(2), half(2),
            full(1), half(3), half(3), full(1), half(3), half(3), half(1), half(1),
            pltpu.SemaphoreType.DMA((copies,)),
            pltpu.SemaphoreType.DMA((copies,)),
            pltpu.SemaphoreType.DMA((2,)),
        ],
        compiler_params=pltpu.CompilerParams(
            collective_id=0, has_side_effects=True, vmem_limit_bytes=48 * 2**20
        ),
        cost_estimate=pl.CostEstimate(
            flops=18 * 96 * 1536 * 1152, bytes_accessed=8 * 96 * 1152 * 2, transcendentals=3 * 96 * 1536
        ),
    )(logit_scale, logit_bias, image_embeds, text_embeds)
    gain = logit_scale[0]
    return (gain * image_total, gain * text_total)


def solution(mesh):
    in_specs = (P(("gx", "gy"), None), P(("gx", "gy"), None), P(), P())
    out_specs = (P(("gx", "gy"), None), P(("gx", "gy"), None))
    return jax.shard_map(body, mesh=mesh, in_specs=in_specs, out_specs=out_specs, check_vma=False)
```

```python
import jax
import jax.numpy as jnp
from jax import lax
from jax.experimental import pallas as pl
from jax.experimental.pallas import tpu as pltpu
from jax.sharding import PartitionSpec as P

MESH = pl.DeviceIdType.MESH
CHUNKS = (16, 16, 16, 16, 16, 16)
RELAYED = 48
CHIPS_X = 4
NT = (((1,), (1,)), ((), ()))
TN = (((0,), (0,)), ((), ()))


def kernel(
    gain_ref, bias_ref, image_ref, text_ref,
    image_out, text_out,
    texts, near, far, text_sum, text_in, text_send, text_back,
    relay, near_own, near_send, near_in, far_own, far_send, far_in, back_send, back_in,
    send_sems, recv_sems, local_sems,
):
    rows, width = image_ref.shape
    group_count = lax.axis_size("gx")
    plane_count = 2 * group_count
    here_x = lax.axis_index("gx")
    here_y = lax.axis_index("gy")
    core = here_y % 2
    chip = here_y // 4
    plane = here_x + group_count * ((here_y // 2) % 2)

    def device(plane_step, chip_step, other_core=False):
        to_plane = (plane + plane_step + plane_count) % plane_count
        to_chip = (chip + chip_step) % CHIPS_X
        to_core = 1 - core if other_core else core
        return (to_plane % group_count, to_chip * 4 + (to_plane // group_count) * 2 + to_core)

    mate = device(0, 0, True)
    across = device(group_count, 0)
    above = device(1, 0)
    below = device(-1, 0)
    line = plane % 4
    here_z = plane // 4

    def at_plane(line_step, z_step):
        to_line = (line + line_step + 4) % 4
        to_z = (here_z + z_step + plane_count // 4) % (plane_count // 4)
        to_plane = 4 * to_z + to_line
        return (to_plane % group_count, chip * 4 + (to_plane // group_count) * 2 + core)

    line_up, line_down = at_plane(1, 0), at_plane(-1, 0)
    z_up, z_down = at_plane(0, 1), at_plane(0, -1)
    side = {step: device(0, step) for step in (1, 3, 2)}

    barrier = pltpu.get_barrier_semaphore()
    partners = [across, above, below, side[1], side[2], side[3], mate, line_up, line_down, z_up, z_down]
    for partner in partners:
        pl.semaphore_signal(barrier, inc=1, device_id=partner, device_id_type=MESH)

    used = [0]
    started = []

    def send(source, target, to):
        slot = used[0]
        used[0] += 1
        copy = pltpu.make_async_remote_copy(
            src_ref=source, dst_ref=target, send_sem=send_sems.at[slot], recv_sem=recv_sems.at[slot],
            device_id=to, device_id_type=MESH,
        )
        copy.start()
        started.append(copy)
        return copy

    def block(ref, at, count=rows):
        return ref.at[pl.ds(at, count)]

    def remote(source, target, send_at, recv_at, to):
        return pltpu.make_async_remote_copy(
            src_ref=source, dst_ref=target, send_sem=send_sems.at[send_at], recv_sem=recv_sems.at[recv_at],
            device_id=to, device_id_type=MESH,
        )

    relays = []

    def shift(source, target, upward):
        to_plane, same_z, at_z = (above, line_up, z_up) if upward else (below, line_down, z_down)
        leaves, passes = (line == 3, line == 0) if upward else (line == 0, line == 3)
        stop = block(relay, len(relays) * RELAYED, RELAYED)
        straight = send(block(source, 0, rows - RELAYED), block(target, 0, rows - RELAYED), to_plane)
        first, second = used[0], used[0] + 1
        used[0] += 2
        part = block(source, rows - RELAYED, RELAYED)
        rest = block(target, rows - RELAYED, RELAYED)
        plain = remote(part, rest, first, first, to_plane)
        detour = remote(part, stop, first, second, same_z)
        onward = remote(stop, rest, second, first, at_z)
        pl.when(jnp.logical_not(leaves))(plain.start)
        pl.when(leaves)(detour.start)
        relays.append(None)

        def pass_on():
            @pl.when(passes)
            def _():
                detour.wait_recv()
                onward.start()

        def arrived():
            straight.wait_recv()
            plain.wait_recv()

        def sent():
            plain.wait_send()
            pl.when(passes)(onward.wait_send)

        return pass_on, arrived, sent

    starts = [sum(CHUNKS[:k]) for k in range(len(CHUNKS))]
    own_text = pltpu.make_async_copy(text_ref, block(texts, 0), local_sems.at[0])
    own_image = pltpu.make_async_copy(image_ref, block(near, 0), local_sems.at[1])
    own_text.start()
    own_image.start()
    pl.semaphore_wait(barrier, len(partners))

    def go_out(k):
        at, count = starts[k], CHUNKS[k]
        return send(block(image_ref, at, count), block(far, 4 * at, count), across)

    outward = [go_out(0)]
    up = shift(text_ref, block(texts, 2 * rows), True)
    down = shift(text_ref, block(texts, rows), False)
    to_mate = send(text_ref, block(texts, 3 * rows), mate)
    spread = [send(image_ref, block(near, (4 - step) * rows), side[step]) for step in side]

    up[0]()
    down[0]()
    up[1]()
    passed_up = send(block(texts, 2 * rows), block(texts, 5 * rows), mate)
    down[1]()
    passed_down = send(block(texts, rows), block(texts, 4 * rows), mate)
    outward += [go_out(k) for k in range(1, len(CHUNKS))]

    gathers = {}

    def gather(k):
        at, count = starts[k], CHUNKS[k]
        outward[k].wait_recv()
        gathers[k] = [
            send(block(far, 4 * at, count), block(far, 4 * at + (4 - step) * count, count), side[step])
            for step in side
        ]

    gain = gain_ref[0]
    bias = bias_ref[0]

    def weights_of(images, own):
        logits = lax.dot_general(images, texts[...], NT, preferred_element_type=jnp.float32)
        weights = jax.nn.sigmoid(gain * logits + bias)
        if own:
            row = lax.broadcasted_iota(jnp.int32, logits.shape, 0)
            column = lax.broadcasted_iota(jnp.int32, logits.shape, 1)
            weights = weights - jnp.logical_and(row == column, row < rows).astype(jnp.float32)
        return weights.astype(jnp.bfloat16)

    gather(0)
    own_text.wait()
    own_image.wait()
    for copy in spread + [to_mate, passed_up, passed_down]:
        copy.wait_recv()

    images = near[...]
    weights = weights_of(images, True)
    text_sum[...] = lax.dot_general(weights, images, TN, preferred_element_type=jnp.float32)
    partial = jnp.dot(weights, texts[...], preferred_element_type=jnp.float32)
    near_own[...] = partial[:rows]
    near_send[...] = partial[rows:].astype(jnp.bfloat16)

    scatters = {}
    returns = {}

    def work(k):
        at, count = starts[k], CHUNKS[k]
        for copy in gathers[k]:
            copy.wait_recv()
        images = far[pl.ds(4 * at, 4 * count), :]
        weights = weights_of(images, False)
        partial = jnp.dot(weights, texts[...], preferred_element_type=jnp.float32)
        far_own[pl.ds(at, count), :] = partial[:count]
        far_send[pl.ds(3 * at, 3 * count), :] = partial[count:].astype(jnp.bfloat16)
        scatters[k] = [
            send(
                block(far_send, 3 * at + (step - 1) * count, count),
                block(far_in, 3 * at + (3 - step) * count, count),
                side[step],
            )
            for step in side
        ]
        text_sum[...] += lax.dot_general(weights, images, TN, preferred_element_type=jnp.float32)

    def give_back(k):
        at, count = starts[k], CHUNKS[k]
        for copy in scatters[k]:
            copy.wait_recv()
        total = far_own[pl.ds(at, count), :]
        for step in range(3):
            total = total + far_in[pl.ds(3 * at + step * count, count), :].astype(jnp.float32)
        back_send[pl.ds(at, count), :] = total.astype(jnp.bfloat16)
        returns[k] = send(block(back_send, at, count), block(back_in, at, count), across)

    last = len(CHUNKS) - 1
    if last >= 1:
        gather(1)
    for k in range(last + 1):
        work(k)
        if k + 2 <= last:
            gather(k + 2)
        if k >= 1:
            give_back(k - 1)
    to_core = send(block(text_sum, 3 * rows, 3 * rows), text_in, mate)
    near_scatter = [
        send(block(near_send, (step - 1) * rows), block(near_in, (3 - step) * rows), side[step]) for step in side
    ]
    give_back(last)

    to_core.wait_recv()
    for step in (0, 1):
        part = pl.ds((step + 1) * rows, rows)
        text_send[pl.ds(step * rows, rows), :] = (text_sum[part, :] + text_in[part, :]).astype(jnp.bfloat16)
    text_up = shift(block(text_send, 0), block(text_back, 0), True)
    text_down = shift(block(text_send, rows), block(text_back, rows), False)

    for copy in near_scatter:
        copy.wait_recv()
    total = near_own[...]
    for step in range(3):
        total = total + near_in[pl.ds(step * rows, rows), :].astype(jnp.float32)
    near_own[...] = total

    text_up[0]()
    text_down[0]()
    text_up[1]()
    text_down[1]()
    text_out[...] = (
        text_sum[pl.ds(0, rows), :]
        + text_in[pl.ds(0, rows), :]
        + text_back[pl.ds(0, rows), :].astype(jnp.float32)
        + text_back[pl.ds(rows, rows), :].astype(jnp.float32)
    )
    for k in range(last + 1):
        part = pl.ds(starts[k], CHUNKS[k])
        returns[k].wait_recv()
        image_out[part, :] = near_own[part, :] + back_in[part, :].astype(jnp.float32)
    for copy in started:
        copy.wait_send()
    for move in (up, down, text_up, text_down):
        move[2]()


def body(image_embeds, text_embeds, logit_scale, logit_bias):
    rows, width = image_embeds.shape
    copies = len(CHUNKS) + 12 + 3 + 3 + 3 * len(CHUNKS) * 2 + len(CHUNKS) + 1 + 3 + 2
    half = lambda count: pltpu.VMEM((count * rows, width), jnp.bfloat16)
    full = lambda count: pltpu.VMEM((count * rows, width), jnp.float32)
    smem = pl.BlockSpec(memory_space=pltpu.SMEM)
    anywhere = pl.BlockSpec(memory_space=pltpu.HBM)
    vmem = pl.BlockSpec(memory_space=pltpu.VMEM)
    image_total, text_total = pl.pallas_call(
        kernel,
        out_shape=[jax.ShapeDtypeStruct((rows, width), jnp.float32)] * 2,
        in_specs=[smem, smem, anywhere, anywhere],
        out_specs=[vmem, vmem],
        scratch_shapes=[
            half(6), half(4), half(4), full(6), full(3), half(2), half(2),
            half(2), full(1), half(3), half(3), full(1), half(3), half(3), half(1), half(1),
            pltpu.SemaphoreType.DMA((copies,)),
            pltpu.SemaphoreType.DMA((copies,)),
            pltpu.SemaphoreType.DMA((2,)),
        ],
        compiler_params=pltpu.CompilerParams(
            collective_id=0, has_side_effects=True, vmem_limit_bytes=48 * 2**20
        ),
        cost_estimate=pl.CostEstimate(
            flops=18 * 96 * 1536 * 1152, bytes_accessed=8 * 96 * 1152 * 2, transcendentals=3 * 96 * 1536
        ),
    )(logit_scale, logit_bias, image_embeds, text_embeds)
    gain = logit_scale[0]
    return (gain * image_total, gain * text_total)


def solution(mesh):
    in_specs = (P(("gx", "gy"), None), P(("gx", "gy"), None), P(), P())
    out_specs = (P(("gx", "gy"), None), P(("gx", "gy"), None))
    return jax.shard_map(body, mesh=mesh, in_specs=in_specs, out_specs=out_specs, check_vma=False)
```

```python
import jax
import jax.numpy as jnp
from jax import lax
from jax.experimental import pallas as pl
from jax.experimental.pallas import tpu as pltpu
from jax.sharding import PartitionSpec as P

MESH = pl.DeviceIdType.MESH
CHUNKS = (16, 16, 16, 16, 16, 16)
RELAYED = 48
RELAYED_LATE = 48
CHIPS_X = 4
NT = (((1,), (1,)), ((), ()))
TN = (((0,), (0,)), ((), ()))


def kernel(
    gain_ref, bias_ref, image_ref, text_ref,
    image_out, text_out,
    texts, near, far, text_sum, text_in, core_send, core_in, text_send, text_back,
    relay, near_own, near_send, near_in, far_own, far_send, far_in, back_send, back_in,
    send_sems, recv_sems, local_sems,
):
    rows, width = image_ref.shape
    group_count = lax.axis_size("gx")
    plane_count = 2 * group_count
    here_x = lax.axis_index("gx")
    here_y = lax.axis_index("gy")
    core = here_y % 2
    chip = here_y // 4
    plane = here_x + group_count * ((here_y // 2) % 2)

    def device(plane_step, chip_step, other_core=False):
        to_plane = (plane + plane_step + plane_count) % plane_count
        to_chip = (chip + chip_step) % CHIPS_X
        to_core = 1 - core if other_core else core
        return (to_plane % group_count, to_chip * 4 + (to_plane // group_count) * 2 + to_core)

    mate = device(0, 0, True)
    across = device(group_count, 0)
    above = device(1, 0)
    below = device(-1, 0)
    line = plane % 4
    here_z = plane // 4

    def at_plane(line_step, z_step):
        to_line = (line + line_step + 4) % 4
        to_z = (here_z + z_step + plane_count // 4) % (plane_count // 4)
        to_plane = 4 * to_z + to_line
        return (to_plane % group_count, chip * 4 + (to_plane // group_count) * 2 + core)

    line_up, line_down = at_plane(1, 0), at_plane(-1, 0)
    z_up, z_down = at_plane(0, 1), at_plane(0, -1)
    skip_up, skip_down = at_plane(2, 1), at_plane(2, -1)
    side = {step: device(0, step) for step in (1, 3, 2)}

    barrier = pltpu.get_barrier_semaphore()
    partners = [across, above, below, side[1], side[2], side[3], mate, line_up, line_down, z_up, z_down, skip_up, skip_down]
    for partner in partners:
        pl.semaphore_signal(barrier, inc=1, device_id=partner, device_id_type=MESH)

    used = [0]
    started = []

    def prepare(source, target, to):
        slot = used[0]
        used[0] += 1
        copy = pltpu.make_async_remote_copy(
            src_ref=source, dst_ref=target, send_sem=send_sems.at[slot], recv_sem=recv_sems.at[slot],
            device_id=to, device_id_type=MESH,
        )
        started.append(copy)
        return copy

    def send(source, target, to):
        copy = prepare(source, target, to)
        copy.start()
        return copy

    def block(ref, at, count=rows):
        return ref.at[pl.ds(at, count)]

    def remote(source, target, send_at, recv_at, to):
        return pltpu.make_async_remote_copy(
            src_ref=source, dst_ref=target, send_sem=send_sems.at[send_at], recv_sem=recv_sems.at[recv_at],
            device_id=to, device_id_type=MESH,
        )

    relays = []

    def shift(source, target, upward, late):
        count = RELAYED_LATE if late else RELAYED
        if late:
            to_plane, first_stop, onward_to = (above, line_down, skip_up) if upward else (below, line_up, skip_down)
        else:
            to_plane, first_stop, onward_to = (above, line_up, z_up) if upward else (below, line_down, z_down)
        leaves = line == (3 if upward else 0)
        passes = line == ((2 if upward else 1) if late else (0 if upward else 3))
        stop = block(relay, sum(relays), count)
        straight = None
        if count < rows:
            straight = send(block(source, 0, rows - count), block(target, 0, rows - count), to_plane)
        first, second = used[0], used[0] + 1
        used[0] += 2
        part = block(source, rows - count, count)
        rest = block(target, rows - count, count)
        plain = remote(part, rest, first, first, to_plane)
        detour = remote(part, stop, first, second, first_stop)
        onward = remote(stop, rest, second, first, onward_to)
        pl.when(jnp.logical_not(leaves))(plain.start)
        pl.when(leaves)(detour.start)
        relays.append(count)

        def pass_on():
            @pl.when(passes)
            def _():
                detour.wait_recv()
                onward.start()

        def arrived():
            if straight is not None:
                straight.wait_recv()
            plain.wait_recv()

        def sent():
            plain.wait_send()
            pl.when(passes)(onward.wait_send)

        return pass_on, arrived, sent

    starts = [sum(CHUNKS[:k]) for k in range(len(CHUNKS))]
    own_text = pltpu.make_async_copy(text_ref, block(texts, 0), local_sems.at[0])
    own_image = pltpu.make_async_copy(image_ref, block(near, 0), local_sems.at[1])
    own_text.start()
    own_image.start()
    pl.semaphore_wait(barrier, len(partners))

    def go_out(k):
        at, count = starts[k], CHUNKS[k]
        return prepare(block(image_ref, at, count), block(far, 4 * at, count), across)

    outward = [go_out(k) for k in range(len(CHUNKS))]

    def further_out(k):
        outward[k].start()

    further_out(0)
    further_out(1)
    up = shift(text_ref, block(texts, 2 * rows), True, False)
    down = shift(text_ref, block(texts, rows), False, False)
    to_mate = send(text_ref, block(texts, 3 * rows), mate)
    spread = [send(image_ref, block(near, (4 - step) * rows), side[step]) for step in side]

    gathers = {}

    def gather(k):
        at, count = starts[k], CHUNKS[k]
        outward[k].wait_recv()
        gathers[k] = [
            send(block(far, 4 * at, count), block(far, 4 * at + (4 - step) * count, count), side[step])
            for step in side
        ]

    gain = gain_ref[0]
    bias = bias_ref[0]

    def weights_of(images, own):
        logits = lax.dot_general(images, texts[...], NT, preferred_element_type=jnp.float32)
        weights = jax.nn.sigmoid(gain * logits + bias)
        if own:
            row = lax.broadcasted_iota(jnp.int32, logits.shape, 0)
            column = lax.broadcasted_iota(jnp.int32, logits.shape, 1)
            weights = weights - jnp.logical_and(row == column, row < rows).astype(jnp.float32)
        return weights.astype(jnp.bfloat16)

    scatters = {}
    returns = {}

    def work(k):
        at, count = starts[k], CHUNKS[k]
        for copy in gathers[k]:
            copy.wait_recv()
        images = far[pl.ds(4 * at, 4 * count), :]
        weights = weights_of(images, False)
        partial = jnp.dot(weights, texts[...], preferred_element_type=jnp.float32)
        far_own[pl.ds(at, count), :] = partial[:count]
        far_send[pl.ds(3 * at, 3 * count), :] = partial[count:].astype(jnp.bfloat16)
        scatters[k] = [
            send(
                block(far_send, 3 * at + (step - 1) * count, count),
                block(far_in, 3 * at + (3 - step) * count, count),
                side[step],
            )
            for step in side
        ]
        text_sum[...] += lax.dot_general(weights, images, TN, preferred_element_type=jnp.float32)

    def give_back(k):
        at, count = starts[k], CHUNKS[k]
        for copy in scatters[k]:
            copy.wait_recv()
        total = far_own[pl.ds(at, count), :]
        for step in range(3):
            total = total + far_in[pl.ds(3 * at + step * count, count), :].astype(jnp.float32)
        back_send[pl.ds(at, count), :] = total.astype(jnp.bfloat16)
        returns[k] = send(block(back_send, at, count), block(back_in, at, count), across)

    last = len(CHUNKS) - 1
    held = {}

    def pass_on():
        up[0]()
        down[0]()

    def text_from_below():
        up[1]()
        held["up"] = send(block(texts, 2 * rows), block(texts, 5 * rows), mate)

    def text_from_above():
        down[1]()
        held["down"] = send(block(texts, rows), block(texts, 4 * rows), mate)

    def work_near():
        own_text.wait()
        own_image.wait()
        for copy in spread + [to_mate, held["up"], held["down"]]:
            copy.wait_recv()
        images = near[...]
        weights = weights_of(images, True)
        partial = jnp.dot(weights, texts[...], preferred_element_type=jnp.float32)
        near_own[...] = partial[:rows]
        near_send[...] = partial[rows:].astype(jnp.bfloat16)
        text_sum[...] = lax.dot_general(weights, images, TN, preferred_element_type=jnp.float32)

    def near_scatter():
        held["near"] = [
            send(block(near_send, (step - 1) * rows), block(near_in, (3 - step) * rows), side[step]) for step in side
        ]

    def text_to_core():
        core_send[...] = text_sum[pl.ds(4 * rows, 2 * rows), :].astype(jnp.bfloat16)
        held["core"] = send(core_send, core_in, mate)
        held["core_own"] = send(block(text_sum, 3 * rows), text_in, mate)

    moves = []

    def text_moves():
        held["core"].wait_recv()
        for step in (0, 1):
            part = pl.ds((step + 1) * rows, rows)
            text_send[pl.ds(step * rows, rows), :] = (
                text_sum[part, :] + core_in[pl.ds(step * rows, rows), :].astype(jnp.float32)
            ).astype(jnp.bfloat16)
            moves.append(shift(block(text_send, step * rows), block(text_back, step * rows), step == 0, True))

    def text_pass_on():
        for move in moves:
            move[0]()

    def near_sum():
        for copy in held["near"]:
            copy.wait_recv()
        total = near_own[...]
        for step in range(3):
            total = total + near_in[pl.ds(step * rows, rows), :].astype(jnp.float32)
        near_own[...] = total

    pass_on()
    text_from_below()
    text_from_above()
    further_out(2)
    further_out(3)
    further_out(4)
    further_out(5)
    gather(0)
    gather(1)
    work_near()
    gather(2)
    work(0)
    gather(3)
    work(1)
    give_back(0)
    gather(4)
    work(2)
    give_back(1)
    gather(5)
    work(3)
    give_back(2)
    work(4)
    give_back(3)
    work(5)
    text_to_core()
    give_back(4)
    near_scatter()
    text_moves()
    give_back(5)
    text_pass_on()
    near_sum()

    held["core_own"].wait_recv()
    for move in moves:
        move[1]()
    text_out[...] = (
        text_sum[pl.ds(0, rows), :]
        + text_in[...]
        + text_back[pl.ds(0, rows), :].astype(jnp.float32)
        + text_back[pl.ds(rows, rows), :].astype(jnp.float32)
    )
    for k in range(last + 1):
        part = pl.ds(starts[k], CHUNKS[k])
        returns[k].wait_recv()
        image_out[part, :] = near_own[part, :] + back_in[part, :].astype(jnp.float32)
    for copy in started:
        copy.wait_send()
    for move in (up, down, *moves):
        move[2]()


def body(image_embeds, text_embeds, logit_scale, logit_bias):
    rows, width = image_embeds.shape
    copies = len(CHUNKS) + 12 + 3 + 3 + 3 * len(CHUNKS) * 2 + len(CHUNKS) + 1 + 3 + 2 + 1
    half = lambda count: pltpu.VMEM((count * rows, width), jnp.bfloat16)
    full = lambda count: pltpu.VMEM((count * rows, width), jnp.float32)
    smem = pl.BlockSpec(memory_space=pltpu.SMEM)
    anywhere = pl.BlockSpec(memory_space=pltpu.HBM)
    vmem = pl.BlockSpec(memory_space=pltpu.VMEM)
    image_total, text_total = pl.pallas_call(
        kernel,
        out_shape=[jax.ShapeDtypeStruct((rows, width), jnp.float32)] * 2,
        in_specs=[smem, smem, anywhere, anywhere],
        out_specs=[vmem, vmem],
        scratch_shapes=[
            half(6), half(4), half(4), full(6), full(1), half(2), half(2), half(2), half(2),
            half(3), full(1), half(3), half(3), full(1), half(3), half(3), half(1), half(1),
            pltpu.SemaphoreType.DMA((copies,)),
            pltpu.SemaphoreType.DMA((copies,)),
            pltpu.SemaphoreType.DMA((2,)),
        ],
        compiler_params=pltpu.CompilerParams(
            collective_id=0, has_side_effects=True, vmem_limit_bytes=48 * 2**20
        ),
        cost_estimate=pl.CostEstimate(
            flops=18 * 96 * 1536 * 1152, bytes_accessed=8 * 96 * 1152 * 2, transcendentals=3 * 96 * 1536
        ),
    )(logit_scale, logit_bias, image_embeds, text_embeds)
    gain = logit_scale[0]
    return (gain * image_total, gain * text_total)


def solution(mesh):
    in_specs = (P(("gx", "gy"), None), P(("gx", "gy"), None), P(), P())
    out_specs = (P(("gx", "gy"), None), P(("gx", "gy"), None))
    return jax.shard_map(body, mesh=mesh, in_specs=in_specs, out_specs=out_specs, check_vma=False)
```

```python
import jax
import jax.numpy as jnp
from jax import lax
from jax.experimental import pallas as pl
from jax.experimental.pallas import tpu as pltpu
from jax.sharding import PartitionSpec as P

MESH = pl.DeviceIdType.MESH
CHUNKS = (16, 16, 16, 16, 16, 16)
RELAYED = 48
RELAYED_LATE = 48
CHIPS_X = 4
NT = (((1,), (1,)), ((), ()))
TN = (((0,), (0,)), ((), ()))


def kernel(
    gain_ref, bias_ref, image_ref, text_ref,
    image_out, text_out,
    texts, near, far, text_sum, text_in, core_send, core_in, text_send, text_back,
    relay, near_own, near_send, near_in, far_own, far_send, far_in, back_send, back_in,
    send_sems, recv_sems, local_sems,
):
    rows, width = image_ref.shape
    group_count = lax.axis_size("gx")
    plane_count = 2 * group_count
    here_x = lax.axis_index("gx")
    here_y = lax.axis_index("gy")
    core = here_y % 2
    chip = here_y // 4
    plane = here_x + group_count * ((here_y // 2) % 2)

    def device(plane_step, chip_step, other_core=False):
        to_plane = (plane + plane_step + plane_count) % plane_count
        to_chip = (chip + chip_step) % CHIPS_X
        to_core = 1 - core if other_core else core
        return (to_plane % group_count, to_chip * 4 + (to_plane // group_count) * 2 + to_core)

    mate = device(0, 0, True)
    across = device(group_count, 0)
    above = device(1, 0)
    below = device(-1, 0)
    line = plane % 4
    here_z = plane // 4

    def at_plane(line_step, z_step):
        to_line = (line + line_step + 4) % 4
        to_z = (here_z + z_step + plane_count // 4) % (plane_count // 4)
        to_plane = 4 * to_z + to_line
        return (to_plane % group_count, chip * 4 + (to_plane // group_count) * 2 + core)

    line_up, line_down = at_plane(1, 0), at_plane(-1, 0)
    z_up, z_down = at_plane(0, 1), at_plane(0, -1)
    skip_up, skip_down = at_plane(2, 1), at_plane(2, -1)
    side = {step: device(0, step) for step in (1, 3, 2)}

    barrier = pltpu.get_barrier_semaphore()
    partners = [across, above, below, side[1], side[2], side[3], mate, line_up, line_down, z_up, z_down, skip_up, skip_down]
    for partner in partners:
        pl.semaphore_signal(barrier, inc=1, device_id=partner, device_id_type=MESH)

    used = [0]
    started = []

    def prepare(source, target, to):
        slot = used[0]
        used[0] += 1
        copy = pltpu.make_async_remote_copy(
            src_ref=source, dst_ref=target, send_sem=send_sems.at[slot], recv_sem=recv_sems.at[slot],
            device_id=to, device_id_type=MESH,
        )
        started.append(copy)
        return copy

    def send(source, target, to):
        copy = prepare(source, target, to)
        copy.start()
        return copy

    def block(ref, at, count=rows):
        return ref.at[pl.ds(at, count)]

    def remote(source, target, send_at, recv_at, to):
        return pltpu.make_async_remote_copy(
            src_ref=source, dst_ref=target, send_sem=send_sems.at[send_at], recv_sem=recv_sems.at[recv_at],
            device_id=to, device_id_type=MESH,
        )

    relays = []

    def shift(source, target, upward, late):
        count = RELAYED_LATE if late else RELAYED
        if late:
            to_plane, first_stop, onward_to = (above, line_down, skip_up) if upward else (below, line_up, skip_down)
        else:
            to_plane, first_stop, onward_to = (above, line_up, z_up) if upward else (below, line_down, z_down)
        leaves = line == (3 if upward else 0)
        passes = line == ((2 if upward else 1) if late else (0 if upward else 3))
        stop = block(relay, sum(relays), count)
        straight = None
        if count < rows:
            straight = send(block(source, 0, rows - count), block(target, 0, rows - count), to_plane)
        first, second = used[0], used[0] + 1
        used[0] += 2
        part = block(source, rows - count, count)
        rest = block(target, rows - count, count)
        plain = remote(part, rest, first, first, to_plane)
        detour = remote(part, stop, first, second, first_stop)
        onward = remote(stop, rest, second, first, onward_to)
        pl.when(jnp.logical_not(leaves))(plain.start)
        pl.when(leaves)(detour.start)
        relays.append(count)

        def pass_on():
            @pl.when(passes)
            def _():
                detour.wait_recv()
                onward.start()

        def arrived():
            if straight is not None:
                straight.wait_recv()
            plain.wait_recv()

        def sent():
            plain.wait_send()
            pl.when(passes)(onward.wait_send)

        return pass_on, arrived, sent

    starts = [sum(CHUNKS[:k]) for k in range(len(CHUNKS))]
    own_text = pltpu.make_async_copy(text_ref, block(texts, 0), local_sems.at[0])
    own_image = pltpu.make_async_copy(image_ref, block(near, 0), local_sems.at[1])
    own_text.start()
    own_image.start()
    pl.semaphore_wait(barrier, len(partners))

    def go_out(k):
        at, count = starts[k], CHUNKS[k]
        return prepare(block(image_ref, at, count), block(far, 4 * at, count), across)

    outward = [go_out(k) for k in range(len(CHUNKS))]

    def further_out(k):
        outward[k].start()

    further_out(0)
    further_out(1)
    up = shift(text_ref, block(texts, 2 * rows), True, False)
    down = shift(text_ref, block(texts, rows), False, False)
    to_mate = send(text_ref, block(texts, 3 * rows), mate)
    spread = [send(image_ref, block(near, (4 - step) * rows), side[step]) for step in side]

    gathers = {}

    def gather(k):
        at, count = starts[k], CHUNKS[k]
        outward[k].wait_recv()
        gathers[k] = [
            send(block(far, 4 * at, count), block(far, 4 * at + (4 - step) * count, count), side[step])
            for step in side
        ]

    gain = gain_ref[0]
    bias = bias_ref[0]

    def weights_of(images, own):
        logits = lax.dot_general(images, texts[...], NT, preferred_element_type=jnp.float32)
        weights = jax.nn.sigmoid(gain * logits + bias)
        if own:
            row = lax.broadcasted_iota(jnp.int32, logits.shape, 0)
            column = lax.broadcasted_iota(jnp.int32, logits.shape, 1)
            weights = weights - jnp.logical_and(row == column, row < rows).astype(jnp.float32)
        return weights.astype(jnp.bfloat16)

    scatters = {}
    returns = {}

    def work(k):
        at, count = starts[k], CHUNKS[k]
        for copy in gathers[k]:
            copy.wait_recv()
        images = far[pl.ds(4 * at, 4 * count), :]
        weights = weights_of(images, False)
        partial = jnp.dot(weights, texts[...], preferred_element_type=jnp.float32)
        far_own[pl.ds(at, count), :] = partial[:count]
        far_send[pl.ds(3 * at, 3 * count), :] = partial[count:].astype(jnp.bfloat16)
        scatters[k] = [
            send(
                block(far_send, 3 * at + (step - 1) * count, count),
                block(far_in, 3 * at + (3 - step) * count, count),
                side[step],
            )
            for step in side
        ]
        text_sum[...] += lax.dot_general(weights, images, TN, preferred_element_type=jnp.float32)

    def give_back(k):
        at, count = starts[k], CHUNKS[k]
        for copy in scatters[k]:
            copy.wait_recv()
        total = far_own[pl.ds(at, count), :]
        for step in range(3):
            total = total + far_in[pl.ds(3 * at + step * count, count), :].astype(jnp.float32)
        back_send[pl.ds(at, count), :] = total.astype(jnp.bfloat16)
        returns[k] = send(block(back_send, at, count), block(back_in, at, count), across)

    last = len(CHUNKS) - 1
    held = {}

    def pass_on():
        up[0]()
        down[0]()

    def text_from_below():
        up[1]()
        held["up"] = send(block(texts, 2 * rows), block(texts, 5 * rows), mate)

    def text_from_above():
        down[1]()
        held["down"] = send(block(texts, rows), block(texts, 4 * rows), mate)

    def work_near():
        own_text.wait()
        own_image.wait()
        for copy in spread + [to_mate, held["up"], held["down"]]:
            copy.wait_recv()
        images = near[...]
        weights = weights_of(images, True)
        partial = jnp.dot(weights, texts[...], preferred_element_type=jnp.float32)
        near_own[...] = partial[:rows]
        near_send[...] = partial[rows:].astype(jnp.bfloat16)
        text_sum[...] = lax.dot_general(weights, images, TN, preferred_element_type=jnp.float32)

    def near_scatter():
        held["near"] = [
            send(block(near_send, (step - 1) * rows), block(near_in, (3 - step) * rows), side[step]) for step in side
        ]

    def text_to_core():
        core_send[...] = text_sum[pl.ds(4 * rows, 2 * rows), :].astype(jnp.bfloat16)
        held["core"] = send(core_send, core_in, mate)
        held["core_own"] = send(block(text_sum, 3 * rows), text_in, mate)

    moves = []

    def text_moves():
        held["core"].wait_recv()
        for step in (0, 1):
            part = pl.ds((step + 1) * rows, rows)
            text_send[pl.ds(step * rows, rows), :] = (
                text_sum[part, :] + core_in[pl.ds(step * rows, rows), :].astype(jnp.float32)
            ).astype(jnp.bfloat16)
            moves.append(shift(block(text_send, step * rows), block(text_back, step * rows), step == 0, True))

    def text_pass_on():
        for move in moves:
            move[0]()

    def near_sum():
        for copy in held["near"]:
            copy.wait_recv()
        total = near_own[...]
        for step in range(3):
            total = total + near_in[pl.ds(step * rows, rows), :].astype(jnp.float32)
        near_own[...] = total

    pass_on()
    further_out(2)
    further_out(3)
    further_out(4)
    further_out(5)
    text_from_below()
    text_from_above()
    gather(0)
    gather(1)
    work_near()
    gather(2)
    work(0)
    gather(3)
    work(1)
    give_back(0)
    gather(4)
    work(2)
    give_back(1)
    gather(5)
    work(3)
    give_back(2)
    work(4)
    give_back(3)
    work(5)
    text_to_core()
    give_back(4)
    near_scatter()
    give_back(5)
    text_moves()
    text_pass_on()
    near_sum()

    held["core_own"].wait_recv()
    for move in moves:
        move[1]()
    text_out[...] = (
        text_sum[pl.ds(0, rows), :]
        + text_in[...]
        + text_back[pl.ds(0, rows), :].astype(jnp.float32)
        + text_back[pl.ds(rows, rows), :].astype(jnp.float32)
    )
    for k in range(last + 1):
        part = pl.ds(starts[k], CHUNKS[k])
        returns[k].wait_recv()
        image_out[part, :] = near_own[part, :] + back_in[part, :].astype(jnp.float32)
    for copy in started:
        copy.wait_send()
    for move in (up, down, *moves):
        move[2]()


def body(image_embeds, text_embeds, logit_scale, logit_bias):
    rows, width = image_embeds.shape
    copies = len(CHUNKS) + 12 + 3 + 3 + 3 * len(CHUNKS) * 2 + len(CHUNKS) + 1 + 3 + 2 + 1
    half = lambda count: pltpu.VMEM((count * rows, width), jnp.bfloat16)
    full = lambda count: pltpu.VMEM((count * rows, width), jnp.float32)
    smem = pl.BlockSpec(memory_space=pltpu.SMEM)
    anywhere = pl.BlockSpec(memory_space=pltpu.HBM)
    vmem = pl.BlockSpec(memory_space=pltpu.VMEM)
    image_total, text_total = pl.pallas_call(
        kernel,
        out_shape=[jax.ShapeDtypeStruct((rows, width), jnp.float32)] * 2,
        in_specs=[smem, smem, anywhere, anywhere],
        out_specs=[vmem, vmem],
        scratch_shapes=[
            half(6), half(4), half(4), full(6), full(1), half(2), half(2), half(2), half(2),
            half(3), full(1), half(3), half(3), full(1), half(3), half(3), half(1), half(1),
            pltpu.SemaphoreType.DMA((copies,)),
            pltpu.SemaphoreType.DMA((copies,)),
            pltpu.SemaphoreType.DMA((2,)),
        ],
        compiler_params=pltpu.CompilerParams(
            collective_id=0, has_side_effects=True, vmem_limit_bytes=48 * 2**20
        ),
        cost_estimate=pl.CostEstimate(
            flops=18 * 96 * 1536 * 1152, bytes_accessed=8 * 96 * 1152 * 2, transcendentals=3 * 96 * 1536
        ),
    )(logit_scale, logit_bias, image_embeds, text_embeds)
    gain = logit_scale[0]
    return (gain * image_total, gain * text_total)


def solution(mesh):
    in_specs = (P(("gx", "gy"), None), P(("gx", "gy"), None), P(), P())
    out_specs = (P(("gx", "gy"), None), P(("gx", "gy"), None))
    return jax.shard_map(body, mesh=mesh, in_specs=in_specs, out_specs=out_specs, check_vma=False)
```

```python
import jax
import jax.numpy as jnp
from jax import lax
from jax.experimental import pallas as pl
from jax.experimental.pallas import tpu as pltpu
from jax.sharding import PartitionSpec as P

MESH = pl.DeviceIdType.MESH
CHUNKS = (16, 16, 16, 16, 16, 16)
RELAYED = 48
RELAYED_LATE = 48
CHIPS_X = 4
NT = (((1,), (1,)), ((), ()))
TN = (((0,), (0,)), ((), ()))


def kernel(
    gain_ref, bias_ref, image_ref, text_ref,
    image_out, text_out,
    texts, near, far, text_sum, text_in, core_send, core_in, text_send, text_back,
    relay, near_own, near_send, near_in, far_own, far_send, far_in, back_send, back_in,
    send_sems, recv_sems, local_sems,
):
    rows, width = image_ref.shape
    group_count = lax.axis_size("gx")
    plane_count = 2 * group_count
    here_x = lax.axis_index("gx")
    here_y = lax.axis_index("gy")
    core = here_y % 2
    chip = here_y // 4
    plane = here_x + group_count * ((here_y // 2) % 2)

    def device(plane_step, chip_step, other_core=False):
        to_plane = (plane + plane_step + plane_count) % plane_count
        to_chip = (chip + chip_step) % CHIPS_X
        to_core = 1 - core if other_core else core
        return (to_plane % group_count, to_chip * 4 + (to_plane // group_count) * 2 + to_core)

    mate = device(0, 0, True)
    across = device(group_count, 0)
    above = device(1, 0)
    below = device(-1, 0)
    line = plane % 4
    here_z = plane // 4

    def at_plane(line_step, z_step):
        to_line = (line + line_step + 4) % 4
        to_z = (here_z + z_step + plane_count // 4) % (plane_count // 4)
        to_plane = 4 * to_z + to_line
        return (to_plane % group_count, chip * 4 + (to_plane // group_count) * 2 + core)

    line_up, line_down = at_plane(1, 0), at_plane(-1, 0)
    z_up, z_down = at_plane(0, 1), at_plane(0, -1)
    skip_up, skip_down = at_plane(2, 1), at_plane(2, -1)
    side = {step: device(0, step) for step in (1, 3, 2)}

    barrier = pltpu.get_barrier_semaphore()
    partners = [across, above, below, side[1], side[2], side[3], mate, line_up, line_down, z_up, z_down, skip_up, skip_down]
    for partner in partners:
        pl.semaphore_signal(barrier, inc=1, device_id=partner, device_id_type=MESH)

    used = [0]
    started = []

    def prepare(source, target, to):
        slot = used[0]
        used[0] += 1
        copy = pltpu.make_async_remote_copy(
            src_ref=source, dst_ref=target, send_sem=send_sems.at[slot], recv_sem=recv_sems.at[slot],
            device_id=to, device_id_type=MESH,
        )
        started.append(copy)
        return copy

    def send(source, target, to):
        copy = prepare(source, target, to)
        copy.start()
        return copy

    def block(ref, at, count=rows):
        return ref.at[pl.ds(at, count)]

    def remote(source, target, send_at, recv_at, to):
        return pltpu.make_async_remote_copy(
            src_ref=source, dst_ref=target, send_sem=send_sems.at[send_at], recv_sem=recv_sems.at[recv_at],
            device_id=to, device_id_type=MESH,
        )

    relays = []

    def shift(source, target, upward, late):
        count = RELAYED_LATE if late else RELAYED
        if late:
            to_plane, first_stop, onward_to = (above, line_down, skip_up) if upward else (below, line_up, skip_down)
        else:
            to_plane, first_stop, onward_to = (above, line_up, z_up) if upward else (below, line_down, z_down)
        leaves = line == (3 if upward else 0)
        passes = line == ((2 if upward else 1) if late else (0 if upward else 3))
        stop = block(relay, sum(relays), count)
        straight = None
        if count < rows:
            straight = send(block(source, 0, rows - count), block(target, 0, rows - count), to_plane)
        first, second = used[0], used[0] + 1
        used[0] += 2
        part = block(source, rows - count, count)
        rest = block(target, rows - count, count)
        plain = remote(part, rest, first, first, to_plane)
        detour = remote(part, stop, first, second, first_stop)
        onward = remote(stop, rest, second, first, onward_to)
        pl.when(jnp.logical_not(leaves))(plain.start)
        pl.when(leaves)(detour.start)
        relays.append(count)

        def pass_on():
            @pl.when(passes)
            def _():
                detour.wait_recv()
                onward.start()

        def arrived():
            if straight is not None:
                straight.wait_recv()
            plain.wait_recv()

        def sent():
            plain.wait_send()
            pl.when(passes)(onward.wait_send)

        return pass_on, arrived, sent

    starts = [sum(CHUNKS[:k]) for k in range(len(CHUNKS))]
    own_text = pltpu.make_async_copy(text_ref, block(texts, 0), local_sems.at[0])
    own_image = pltpu.make_async_copy(image_ref, block(near, 0), local_sems.at[1])
    own_text.start()
    own_image.start()
    pl.semaphore_wait(barrier, len(partners))

    def go_out(k):
        at, count = starts[k], CHUNKS[k]
        return prepare(block(image_ref, at, count), block(far, 4 * at, count), across)

    outward = [go_out(k) for k in range(len(CHUNKS))]

    def further_out(k):
        outward[k].start()

    further_out(0)
    further_out(1)
    up = shift(text_ref, block(texts, 2 * rows), True, False)
    down = shift(text_ref, block(texts, rows), False, False)
    to_mate = send(text_ref, block(texts, 3 * rows), mate)
    spread = [send(image_ref, block(near, (4 - step) * rows), side[step]) for step in side]

    gathers = {}

    def gather(k):
        at, count = starts[k], CHUNKS[k]
        outward[k].wait_recv()
        gathers[k] = [
            send(block(far, 4 * at, count), block(far, 4 * at + (4 - step) * count, count), side[step])
            for step in side
        ]

    gain = gain_ref[0]
    bias = bias_ref[0]

    def weights_of(images, own):
        logits = lax.dot_general(images, texts[...], NT, preferred_element_type=jnp.float32)
        weights = jax.nn.sigmoid(gain * logits + bias)
        if own:
            row = lax.broadcasted_iota(jnp.int32, logits.shape, 0)
            column = lax.broadcasted_iota(jnp.int32, logits.shape, 1)
            weights = weights - jnp.logical_and(row == column, row < rows).astype(jnp.float32)
        return weights.astype(jnp.bfloat16)

    scatters = {}
    returns = {}

    def work(k):
        at, count = starts[k], CHUNKS[k]
        for copy in gathers[k]:
            copy.wait_recv()
        images = far[pl.ds(4 * at, 4 * count), :]
        weights = weights_of(images, False)
        partial = jnp.dot(weights, texts[...], preferred_element_type=jnp.float32)
        far_own[pl.ds(at, count), :] = partial[:count]
        far_send[pl.ds(3 * at, 3 * count), :] = partial[count:].astype(jnp.bfloat16)
        scatters[k] = [
            send(
                block(far_send, 3 * at + (step - 1) * count, count),
                block(far_in, 3 * at + (3 - step) * count, count),
                side[step],
            )
            for step in side
        ]
        text_sum[...] += lax.dot_general(weights, images, TN, preferred_element_type=jnp.float32)

    def give_back(k):
        at, count = starts[k], CHUNKS[k]
        for copy in scatters[k]:
            copy.wait_recv()
        total = far_own[pl.ds(at, count), :]
        for step in range(3):
            total = total + far_in[pl.ds(3 * at + step * count, count), :].astype(jnp.float32)
        back_send[pl.ds(at, count), :] = total.astype(jnp.bfloat16)
        returns[k] = send(block(back_send, at, count), block(back_in, at, count), across)

    last = len(CHUNKS) - 1
    held = {}

    def pass_on():
        up[0]()
        down[0]()

    def text_from_below():
        up[1]()
        held["up"] = send(block(texts, 2 * rows), block(texts, 5 * rows), mate)

    def text_from_above():
        down[1]()
        held["down"] = send(block(texts, rows), block(texts, 4 * rows), mate)

    def work_near():
        own_text.wait()
        own_image.wait()
        for copy in spread + [to_mate, held["up"], held["down"]]:
            copy.wait_recv()
        images = near[...]
        weights = weights_of(images, True)
        partial = jnp.dot(weights, texts[...], preferred_element_type=jnp.float32)
        near_own[...] = partial[:rows]
        near_send[...] = partial[rows:].astype(jnp.bfloat16)
        text_sum[...] = lax.dot_general(weights, images, TN, preferred_element_type=jnp.float32)

    def near_scatter():
        held["near"] = [
            send(block(near_send, (step - 1) * rows), block(near_in, (3 - step) * rows), side[step]) for step in side
        ]

    def text_to_core():
        core_send[...] = text_sum[pl.ds(4 * rows, 2 * rows), :].astype(jnp.bfloat16)
        held["core"] = send(core_send, core_in, mate)
        held["core_own"] = send(block(text_sum, 3 * rows), text_in, mate)

    moves = []

    def text_moves():
        held["core"].wait_recv()
        for step in (0, 1):
            part = pl.ds((step + 1) * rows, rows)
            text_send[pl.ds(step * rows, rows), :] = (
                text_sum[part, :] + core_in[pl.ds(step * rows, rows), :].astype(jnp.float32)
            ).astype(jnp.bfloat16)
            moves.append(shift(block(text_send, step * rows), block(text_back, step * rows), step == 0, True))

    def text_pass_on():
        for move in moves:
            move[0]()

    def near_sum():
        for copy in held["near"]:
            copy.wait_recv()
        total = near_own[...]
        for step in range(3):
            total = total + near_in[pl.ds(step * rows, rows), :].astype(jnp.float32)
        near_own[...] = total

    pass_on()
    further_out(2)
    further_out(3)
    further_out(4)
    further_out(5)
    text_from_below()
    text_from_above()
    gather(0)
    gather(1)
    work_near()
    gather(2)
    work(0)
    gather(3)
    work(1)
    give_back(0)
    gather(4)
    work(2)
    give_back(1)
    gather(5)
    work(3)
    give_back(2)
    work(4)
    give_back(3)
    work(5)
    text_to_core()
    give_back(4)
    give_back(5)
    near_scatter()
    text_moves()
    text_pass_on()
    near_sum()

    held["core_own"].wait_recv()
    for move in moves:
        move[1]()
    text_out[...] = (
        text_sum[pl.ds(0, rows), :]
        + text_in[...]
        + text_back[pl.ds(0, rows), :].astype(jnp.float32)
        + text_back[pl.ds(rows, rows), :].astype(jnp.float32)
    )
    for k in range(last + 1):
        part = pl.ds(starts[k], CHUNKS[k])
        returns[k].wait_recv()
        image_out[part, :] = near_own[part, :] + back_in[part, :].astype(jnp.float32)
    for copy in started:
        copy.wait_send()
    for move in (up, down, *moves):
        move[2]()


def body(image_embeds, text_embeds, logit_scale, logit_bias):
    rows, width = image_embeds.shape
    copies = len(CHUNKS) + 12 + 3 + 3 + 3 * len(CHUNKS) * 2 + len(CHUNKS) + 1 + 3 + 2 + 1
    half = lambda count: pltpu.VMEM((count * rows, width), jnp.bfloat16)
    full = lambda count: pltpu.VMEM((count * rows, width), jnp.float32)
    smem = pl.BlockSpec(memory_space=pltpu.SMEM)
    anywhere = pl.BlockSpec(memory_space=pltpu.HBM)
    vmem = pl.BlockSpec(memory_space=pltpu.VMEM)
    image_total, text_total = pl.pallas_call(
        kernel,
        out_shape=[jax.ShapeDtypeStruct((rows, width), jnp.float32)] * 2,
        in_specs=[smem, smem, anywhere, anywhere],
        out_specs=[vmem, vmem],
        scratch_shapes=[
            half(6), half(4), half(4), full(6), full(1), half(2), half(2), half(2), half(2),
            half(3), full(1), half(3), half(3), full(1), half(3), half(3), half(1), half(1),
            pltpu.SemaphoreType.DMA((copies,)),
            pltpu.SemaphoreType.DMA((copies,)),
            pltpu.SemaphoreType.DMA((2,)),
        ],
        compiler_params=pltpu.CompilerParams(
            collective_id=0, has_side_effects=True, vmem_limit_bytes=48 * 2**20
        ),
        cost_estimate=pl.CostEstimate(
            flops=18 * 96 * 1536 * 1152, bytes_accessed=8 * 96 * 1152 * 2, transcendentals=3 * 96 * 1536
        ),
    )(logit_scale, logit_bias, image_embeds, text_embeds)
    gain = logit_scale[0]
    return (gain * image_total, gain * text_total)


def solution(mesh):
    in_specs = (P(("gx", "gy"), None), P(("gx", "gy"), None), P(), P())
    out_specs = (P(("gx", "gy"), None), P(("gx", "gy"), None))
    return jax.shard_map(body, mesh=mesh, in_specs=in_specs, out_specs=out_specs, check_vma=False)
```
